512 devices in a mesh: row: 128 (over y, z, x_lo), rep: 4 (over x_hi, core).
Axes of the slice: x: 4 (x_hi: 2, x_lo: 2; x = x_hi * 2 + x_lo), y: 4, z: 16, core: 2. Of those that a mesh axis runs over, the one named last changes fastest.
Arguments:
- features: bfloat16 [65536, 128], P(('row', 'rep')), may hold values from -6 to 6
- weight: bfloat16 [128, 256], replicated, may hold values from -0.5 to 0.5
- upstream: bfloat16 [65536, 256], P(('row', 'rep')), may hold values from -6 to 6
- tile_owners: int32 [512, 4, 4], P('row', 'rep'), may hold values from 0 to 127
- tile_counts: int32 [512, 4], P('row', 'rep'), may hold values from 1 to 4, 10 in all within a row
- tile_values: bfloat16 [512, 4, 4, 128, 128], P('row', 'rep'), may hold values from -0.15625 to 0.15625
Outputs:
- hidden: bfloat16 [65536, 256], P(('row', 'rep'))
- grad_weight: float32 [128, 256], replicated
- grad_features: float32 [65536, 128], P(('row', 'rep'))
The draws below stay inside these ranges and needn't reach their ends.
All inputs are finite; a program needn't handle non-finite values. No bound on the sum of `tile_counts` on one device may be relied on, other than what follows from the above.
Results may differ from the reference program's by a relative error of at most 0.0057.
Values may be sent and summed in bfloat16 or wider, within the bound.
No kernel may reach another device: no remote copies, remote signals or barrier semaphores. Data moves between devices by JAX's collectives and lax.ppermute only.
A program may use at most 128 MiB of HBM per device.

```python
import math
import jax
import jax.numpy as jnp
import numpy as np
from jax import lax

F = 128
HID = 256
TILE = 128
MAXT = 4
LIVE = 10
NB = 512
NODES = 65536
N_ROW = 128
N_REP = 4


def with_ends(entries, own_key, low, high):
    extent = entries.shape
    spot = [jax.random.randint(jax.random.fold_in(own_key, axis), (), 0, extent[axis]) for axis in range(len(extent))]
    entries = entries.at[tuple(spot)].set(low)
    longest = extent.index(max(extent))
    spot[longest] = (spot[longest] + 1) % extent[longest]
    return entries.at[tuple(spot)].set(high)


def levels(own_key, shape, cuts, low, high):
    gain, own = 1.0, jax.random.fold_in(own_key, 6)
    for axis_at, blocks in cuts:
        heights = jnp.exp(jax.random.uniform(jax.random.fold_in(own, axis_at), (blocks,), jnp.float32, low / len(cuts), high / len(cuts)))
        gain = gain * jnp.repeat(heights, shape[axis_at] // blocks).reshape([-1 if axis == axis_at else 1 for axis in range(len(shape))])
    return gain


def rank_table(number_of, lean):
    loads = [(1 << 20) // math.isqrt(grade ** lean) + 1 for grade in range(1, number_of + 1)]
    scale = 1 + sum(loads) // (1 << 30)
    return np.cumsum(np.array([max(1, weight // scale) for weight in loads]))


def ranked_ids(own_key, extent, amount, lean):
    grid = rank_table(amount, lean)
    ticket = jax.random.randint(jax.random.fold_in(own_key, 1), extent, 0, int(grid[amount - 1]))
    standing = jnp.searchsorted(jnp.asarray(grid, jnp.int32), ticket, side="right")
    return jax.random.permutation(jax.random.fold_in(own_key, 2), amount)[standing].astype(jnp.int32)


def profile(count, total, reach, skew):
    weights = [(1 << 20) // math.isqrt(grade ** skew) + 1 for grade in range(2, count + 1)]
    rest, holding = total - reach - (count - 1), [1] * (count - 1)
    while rest > 0:
        movable = [i for i in range(count - 1) if holding[i] < reach]
        whole, left = sum([weights[i] for i in movable]), rest
        for i in movable:
            more = min(reach - holding[i], max(1, left * weights[i] // whole), rest)
            holding[i] = holding[i] + more
            rest = rest - more
    return np.array([reach] + holding)


def ragged_sizes(rng, count, total, reach, skew):
    if count == 2:
        one = jax.random.randint(rng, (), max(1, total - reach), min(reach, total - 1) + 1)
        return jnp.stack([one, total - one])
    sizes = jnp.asarray(profile(count, total, reach, skew), jnp.int32)
    pairs = (count - 1) // 2
    giver, sink = sizes[1:1 + 2 * pairs:2], sizes[2:2 + 2 * pairs:2]
    room = jnp.minimum(giver - 1, reach - sink)
    moved = jax.random.randint(jax.random.fold_in(rng, 1), (pairs,), 0, 1 << 20) % (room + 1)
    sizes = sizes.at[1:1 + 2 * pairs:2].set(giver - moved).at[2:2 + 2 * pairs:2].set(sink + moved)
    return sizes[jax.random.permutation(jax.random.fold_in(rng, 2), count)]


def normal_values(rng, dims, deviation, limit, pieces=(), held_as=jnp.bfloat16):
    array = jax.random.normal(rng, dims, jnp.float32) * deviation
    if len(pieces) > 0:
        array = levels(rng, dims, pieces, -0.22, 0.18) * array
    return jnp.clip(array, min=-limit, max=limit).astype(held_as)


def setup_inputs(seed: int = 0) -> dict:
    key_of = jax.random.split(jax.random.key(seed), 7)
    features = normal_values(key_of[0], (NODES, F), 1.0, 6.0, ((0, 512),))
    weight = normal_values(key_of[1], (F, HID), F ** -0.5, 0.5)
    upstream = normal_values(key_of[2], (NODES, HID), 1.0, 6.0, ((0, 512),))
    tile_owners = with_ends(ranked_ids(key_of[3], (NB, N_REP, MAXT), N_ROW, 2), jax.random.fold_in(key_of[3], 3), 0, N_ROW - 1).astype(jnp.int32)
    tile_counts = jax.vmap(lambda own: ragged_sizes(own, N_REP, LIVE, MAXT, 2))(jax.random.split(key_of[4], NB)).reshape((NB, N_REP)).astype(jnp.int32)
    tile_values = normal_values(key_of[5], (NB, N_REP, MAXT, TILE, TILE), (LIVE * TILE) ** -0.5, 0.15625, ((0, 128), (1, 4)))
    return {"features": features, "weight": weight, "upstream": upstream, "tile_owners": tile_owners, "tile_counts": tile_counts, "tile_values": tile_values}


def reference(features, weight, upstream, tile_owners, tile_counts, tile_values):
    node_tiles = features.reshape(NB, TILE, F)
    section_index = jnp.arange(N_REP, dtype=jnp.int32)
    slot_index = jnp.arange(MAXT, dtype=jnp.int32)

    def forward_block(inputs):
        owners, counts, values = inputs
        columns = (owners * N_REP + section_index[:, None]).astype(jnp.int32)
        active = slot_index[None, :] < counts[:, None]
        picked = jnp.where(active[:, :, None, None], node_tiles[columns], jnp.zeros((), jnp.bfloat16))
        return jnp.einsum('stij,stjf->if', values.astype(jnp.float32), picked.astype(jnp.float32))
    aggregated_sum = lax.map(forward_block, (tile_owners, tile_counts, tile_values))
    aggregated = aggregated_sum.reshape(NODES, F).astype(jnp.bfloat16)
    pre_act = jnp.dot(aggregated, weight, preferred_element_type=jnp.float32)
    hidden = jax.nn.gelu(pre_act).astype(jnp.bfloat16)
    unused_value, pullback = jax.vjp(jax.nn.gelu, pre_act)
    slope = pullback(upstream.astype(pre_act.dtype))[0].astype(jnp.bfloat16)
    grad_weight = jnp.dot(aggregated.T, slope, preferred_element_type=jnp.float32)
    back_rows = jnp.dot(slope, weight.T, preferred_element_type=jnp.float32).astype(jnp.bfloat16)
    back_tiles = back_rows.reshape(NB, TILE, F)

    def backward_block(running, inputs):
        owners, counts, values, rows_back = inputs
        columns = (owners * N_REP + section_index[:, None]).astype(jnp.int32)
        active = slot_index[None, :] < counts[:, None]
        parts = jnp.einsum('stji,jf->stif', values.astype(jnp.float32), rows_back.astype(jnp.float32))
        parts = jnp.where(active[:, :, None, None], parts, jnp.zeros((), parts.dtype))
        running = running.at[columns.reshape(-1)].add(parts.reshape(-1, TILE, F))
        return (running, None)
    start_grads = jnp.zeros((NB, TILE, F), jnp.float32)
    grads, unused_rest = lax.scan(backward_block, start_grads, (tile_owners, tile_counts, tile_values, back_tiles))
    return (hidden, grad_weight, grads.reshape(NODES, F))
```

```python
import jax
import jax.numpy as jnp
from jax import lax
from jax.sharding import Mesh, PartitionSpec as P

ROW = ("y", "z", "xl")
REP = ("xh", "c")
PLANE = ("y", "xl")
NY, NZ, NX = 4, 16, 2
NP = NY * NX
TILE = 128
CUT = TILE // NP


def exchange(array, axes):
    return lax.all_to_all(array, axes, split_axis=0, concat_axis=0, tiled=True)


def body(features, weight, upstream, tile_owners, tile_counts, tile_values):
    f32, bf16 = jnp.float32, jnp.bfloat16
    width = features.shape[1]
    owners = tile_owners[:, 0, :]
    counts = tile_counts[:, 0]
    values = tile_values[:, 0]
    blocks, slots = owners.shape
    total = blocks * slots
    active = jnp.arange(slots, dtype=jnp.int32)[None, :] < counts[:, None]
    code = jnp.where(active, owners, -1).reshape(total).astype(bf16)
    code_rows = jnp.broadcast_to(jnp.pad(code, (0, width - total))[None, None, :], (NP, CUT, width))

    first = exchange(jnp.concatenate([features.reshape(NP, CUT, width), code_rows], axis=1), PLANE)
    codes = first[:, CUT, :total].astype(jnp.int32).reshape(NP * total)
    table = exchange(jnp.broadcast_to(first[None, :, :CUT], (NZ, NP, CUT, width)), "z")
    place = jnp.arange(NZ * NP, dtype=jnp.int32)
    ident = ((place // NX) % NY) * (NZ * NX) + (place // NP) * NX + place % NX
    pick = (codes[:, None] == ident[None, :]).astype(bf16)
    wanted = jnp.dot(pick, table.reshape(NZ * NP, CUT * width), preferred_element_type=f32).astype(bf16)
    third = exchange(wanted.reshape(NP, total, CUT, width), PLANE)
    picked = third.transpose(1, 0, 2, 3).reshape(blocks, slots, TILE, width)
    partial_value = jnp.einsum("btij,btjf->bif", values, picked, preferred_element_type=f32).astype(bf16)

    halves = jnp.stack([upstream[:, :width], upstream[:, width:]])
    shared = lax.all_gather(jnp.concatenate([partial_value, halves]), REP, axis=0)
    aggregated = jnp.sum(shared[:, :blocks].astype(f32), axis=0).astype(bf16).reshape(blocks * TILE, width)
    upstream_all = jnp.concatenate([shared[:, blocks], shared[:, blocks + 1]], axis=-1).reshape(blocks * TILE, 2 * width)

    pre_act = jnp.dot(aggregated, weight, preferred_element_type=f32)
    hidden_all, pullback = jax.vjp(jax.nn.gelu, pre_act)
    hidden = lax.dynamic_slice_in_dim(hidden_all.astype(bf16), lax.axis_index(REP) * TILE, TILE, 0)
    slope = pullback(upstream_all.astype(f32))[0].astype(bf16)
    weight_part = jnp.dot(aggregated.T, slope, preferred_element_type=f32)
    back_rows = jnp.dot(slope, weight.T, preferred_element_type=f32).astype(bf16).reshape(blocks, TILE, width)
    parts = jnp.einsum("btji,bjf->btif", values, back_rows, preferred_element_type=f32).astype(bf16)

    parts = parts.reshape(total, NP, CUT, width).transpose(1, 0, 2, 3)
    weight_cut = weight_part.astype(bf16).reshape(NP, CUT, 2, width).transpose(0, 2, 1, 3)
    fifth = exchange(jnp.concatenate([parts, weight_cut], axis=1), PLANE)
    summed = jnp.dot(pick.T, fifth[:, :total].reshape(NP * total, CUT * width), preferred_element_type=f32).astype(bf16)
    weight_sum = jnp.sum(fifth[:, total:].astype(f32), axis=0).astype(bf16)
    sixth = exchange(
        jnp.concatenate(
            [summed.reshape(NZ, NP, CUT, width), jnp.broadcast_to(weight_sum[None], (NZ, 2, CUT, width))], axis=1
        ),
        "z",
    )
    sums = jnp.sum(sixth.astype(f32), axis=0).astype(bf16)
    last = exchange(
        jnp.concatenate([sums[:NP, None], jnp.broadcast_to(sums[None, NP:], (NP, 2, CUT, width))], axis=1), PLANE
    ).astype(f32)
    grad_features = last[:, 0].reshape(TILE, width)
    grad_weight = last[:, 1:].transpose(0, 2, 1, 3).reshape(TILE, 2 * width)
    return (hidden, grad_weight, grad_features)


def solution(mesh):
    parted = Mesh(mesh.devices.reshape(NY, NZ, NX, 2, 2), ROW + REP)
    in_specs = (
        P(ROW + REP, None),
        P(),
        P(ROW + REP, None),
        P(ROW, REP, None),
        P(ROW, REP),
        P(ROW, REP, None, None, None),
    )
    out_specs = (P(ROW + REP, None), P(), P(ROW + REP, None))
    return jax.shard_map(body, mesh=parted, in_specs=in_specs, out_specs=out_specs, check_vma=False)
```

```python
import jax
import jax.numpy as jnp
from jax import lax
from jax.sharding import Mesh, PartitionSpec as P

ROW = ("y", "zq", "zp", "xl")
REP = ("xh", "c")
NEAR = ("y", "zp", "xl")
NY, NQ, NZP, NX = 4, 8, 2, 2
NM = NY * NZP * NX
TILE = 128
CUT = TILE // NM


def exchange(array, axes):
    return lax.all_to_all(array, axes, split_axis=0, concat_axis=0, tiled=True)


def split(array):
    high = lax.reduce_precision(array, 8, 7)
    return jnp.concatenate([high.astype(jnp.bfloat16), (array - high).astype(jnp.bfloat16)])


def body(features, weight, upstream, tile_owners, tile_counts, tile_values):
    f32, bf16 = jnp.float32, jnp.bfloat16
    width = features.shape[1]
    owners = tile_owners[:, 0, :]
    counts = tile_counts[:, 0]
    values = tile_values[:, 0]
    blocks, slots = owners.shape
    total = blocks * slots
    active = jnp.arange(slots, dtype=jnp.int32)[None, :] < counts[:, None]
    code = jnp.where(active, owners, -1).reshape(total).astype(bf16)
    code_rows = jnp.broadcast_to(jnp.pad(code, (0, width - total))[None, None, :], (NM, CUT, width))

    first = exchange(jnp.concatenate([features.reshape(NM, CUT, width), code_rows], axis=1), NEAR)
    codes = first[:, CUT, :total].astype(jnp.int32).reshape(NM * total)
    table = exchange(jnp.broadcast_to(first[None, :, :CUT], (NQ, NM, CUT, width)), "zq")
    place = jnp.arange(NQ * NM, dtype=jnp.int32)
    ident = ((place // (NZP * NX)) % NY) * (NQ * NZP * NX) + (place // NM) * (NZP * NX) + place % (NZP * NX)
    pick = (codes[:, None] == ident[None, :]).astype(bf16)
    wanted = jnp.dot(pick, table.reshape(NQ * NM, CUT * width), preferred_element_type=f32).astype(bf16)
    third = exchange(wanted.reshape(NM, total, CUT, width), NEAR)
    picked = third.transpose(1, 0, 2, 3).reshape(blocks, slots, TILE, width)
    partial_value = jnp.einsum("btij,btjf->bif", values, picked, preferred_element_type=f32)

    pair = lax.all_gather(split(partial_value), "c", axis=0).reshape(2, 2, 2, 2, TILE, width)
    own_half = lax.dynamic_index_in_dim(pair, lax.axis_index("c"), 3, keepdims=False)
    half_sum = jnp.sum(own_half.astype(f32), axis=(0, 1))
    halves = jnp.stack([upstream[:, :width], upstream[:, width:]])
    far = lax.all_gather(jnp.concatenate([split(half_sum), halves]), "xh", axis=0)
    half_total = jnp.sum(far[:, :4].reshape(2, 2, 2, TILE, width).astype(f32), axis=(0, 1)).astype(bf16)
    shared = lax.all_gather(jnp.concatenate([half_total, far[0, 4:], far[1, 4:]]), "c", axis=0)
    aggregated = shared[:, :2].transpose(1, 0, 2, 3).reshape(blocks * TILE, width)
    upstream_all = shared[:, 2:].reshape(2, 2, 2, TILE, width).transpose(1, 0, 3, 2, 4).reshape(blocks * TILE, 2 * width)

    pre_act = jnp.dot(aggregated, weight, preferred_element_type=f32)
    hidden_all, pullback = jax.vjp(jax.nn.gelu, pre_act)
    hidden = lax.dynamic_slice_in_dim(hidden_all.astype(bf16), lax.axis_index(REP) * TILE, TILE, 0)
    slope = pullback(upstream_all.astype(f32))[0].astype(bf16)
    weight_part = jnp.dot(aggregated.T, slope, preferred_element_type=f32)
    back_rows = jnp.dot(slope, weight.T, preferred_element_type=f32).astype(bf16).reshape(blocks, TILE, width)
    parts = jnp.einsum("btji,bjf->btif", values, back_rows, preferred_element_type=f32).astype(bf16)

    parts = parts.reshape(total, NM, CUT, width).transpose(1, 0, 2, 3)
    weight_cut = weight_part.astype(bf16).reshape(NM, CUT, 2, width).transpose(0, 2, 1, 3)
    fifth = exchange(jnp.concatenate([parts, weight_cut], axis=1), NEAR)
    summed = jnp.dot(pick.T, fifth[:, :total].reshape(NM * total, CUT * width), preferred_element_type=f32).astype(bf16)
    weight_sum = jnp.sum(fifth[:, total:].astype(f32), axis=0).astype(bf16)
    sixth = exchange(
        jnp.concatenate(
            [summed.reshape(NQ, NM, CUT, width), jnp.broadcast_to(weight_sum[None], (NQ, 2, CUT, width))], axis=1
        ),
        "zq",
    )
    sums = jnp.sum(sixth.astype(f32), axis=0).astype(bf16)
    last = exchange(
        jnp.concatenate([sums[:NM, None], jnp.broadcast_to(sums[None, NM:], (NM, 2, CUT, width))], axis=1), NEAR
    ).astype(f32)
    grad_features = last[:, 0].reshape(TILE, width)
    grad_weight = last[:, 1:].transpose(0, 2, 1, 3).reshape(TILE, 2 * width)
    return (hidden, grad_weight, grad_features)


def solution(mesh):
    parted = Mesh(mesh.devices.reshape(NY, NQ, NZP, NX, 2, 2), ROW + REP)
    in_specs = (
        P(ROW + REP, None),
        P(),
        P(ROW + REP, None),
        P(ROW, REP, None),
        P(ROW, REP),
        P(ROW, REP, None, None, None),
    )
    out_specs = (P(ROW + REP, None), P(), P(ROW + REP, None))
    return jax.shard_map(body, mesh=parted, in_specs=in_specs, out_specs=out_specs, check_vma=False)
```

```python
import jax
import jax.numpy as jnp
from jax import lax
from jax.sharding import Mesh, PartitionSpec as P

ROW = ("y", "zq", "zp", "xl")
REP = ("xh", "c")
NEAR = ("y", "zp", "xl")
NY, NQ, NZP, NX = 4, 8, 2, 2
NM = NY * NZP * NX
TILE = 128
CUT = TILE // NM


def exchange(array, axes):
    flat = array.reshape(array.shape[0], -1, array.shape[-1])
    return lax.all_to_all(flat, axes, split_axis=0, concat_axis=0, tiled=True).reshape(array.shape)


def split(array):
    high = lax.reduce_precision(array, 8, 7)
    return jnp.concatenate([high.astype(jnp.bfloat16), (array - high).astype(jnp.bfloat16)])


def body(features, weight, upstream, tile_owners, tile_counts, tile_values):
    f32, bf16 = jnp.float32, jnp.bfloat16
    width = features.shape[1]
    owners = tile_owners[:, 0, :]
    counts = tile_counts[:, 0]
    values = tile_values[:, 0]
    blocks, slots = owners.shape
    total = blocks * slots
    active = jnp.arange(slots, dtype=jnp.int32)[None, :] < counts[:, None]
    wide = exchange(jnp.broadcast_to(features[None], (NQ, TILE, width)), "zq")
    code = jnp.where(active, owners, -1).reshape(total).astype(bf16)
    code_rows = jnp.broadcast_to(jnp.pad(code, (0, width - total))[None, None, None, :], (NM, 1, CUT, width))
    halves = jnp.stack([upstream[:, :width], upstream[:, width:]])
    upstream_all = lax.all_gather(lax.all_gather(halves, "xh", axis=0), "c", axis=1)
    wide, code_rows, upstream_all = lax.optimization_barrier((wide, code_rows, upstream_all))

    slices = wide.reshape(NQ, NM, CUT, width).transpose(1, 0, 2, 3)
    second = exchange(jnp.concatenate([slices, code_rows], axis=1), NEAR)
    codes = second[:, NQ, 0, :total].astype(jnp.int32).reshape(NM * total)
    place = jnp.arange(NQ * NM, dtype=jnp.int32)
    member = place // NQ
    ident = (member // (NZP * NX)) * (NQ * NZP * NX) + (place % NQ) * (NZP * NX) + member % (NZP * NX)
    pick = (codes[:, None] == ident[None, :]).astype(bf16)
    table = second[:, :NQ].reshape(NQ * NM, CUT * width)
    wanted = jnp.dot(pick, table, preferred_element_type=f32).astype(bf16)
    third = exchange(wanted.reshape(NM, total, CUT, width), NEAR)
    picked = third.transpose(1, 0, 2, 3).reshape(blocks, slots, TILE, width)
    partial_value = jnp.einsum("btij,btjf->bif", values, picked, preferred_element_type=f32)

    pair = lax.all_gather(split(partial_value), "c", axis=0).reshape(2, 2, 2, 2, TILE, width)
    own_half = lax.dynamic_index_in_dim(pair, lax.axis_index("c"), 3, keepdims=False)
    half_sum = jnp.sum(own_half.astype(f32), axis=(0, 1))
    far = lax.all_gather(split(half_sum), "xh", axis=0)
    half_total = jnp.sum(far.reshape(2, 2, 2, TILE, width).astype(f32), axis=(0, 1)).astype(bf16)
    aggregated = lax.all_gather(half_total, "c", axis=1).reshape(blocks * TILE, width)
    upstream_all = upstream_all.transpose(0, 1, 3, 2, 4).reshape(blocks * TILE, 2 * width)

    pre_act = jnp.dot(aggregated, weight, preferred_element_type=f32)
    hidden_all, pullback = jax.vjp(jax.nn.gelu, pre_act)
    hidden = lax.dynamic_slice_in_dim(hidden_all.astype(bf16), lax.axis_index(REP) * TILE, TILE, 0)
    slope = pullback(upstream_all.astype(f32))[0].astype(bf16)
    weight_part = jnp.dot(aggregated.T, slope, preferred_element_type=f32)
    back_rows = jnp.dot(slope, weight.T, preferred_element_type=f32).astype(bf16).reshape(blocks, TILE, width)
    parts = jnp.einsum("btji,bjf->btif", values, back_rows, preferred_element_type=f32).astype(bf16)

    parts = parts.reshape(total, NM, CUT, width).transpose(1, 0, 2, 3)
    weight_cut = weight_part.astype(bf16).reshape(NM, CUT, 2, width).transpose(0, 2, 1, 3)
    fifth = exchange(jnp.concatenate([parts, weight_cut], axis=1), NEAR)
    summed = jnp.dot(pick.T, fifth[:, :total].reshape(NM * total, CUT * width), preferred_element_type=f32).astype(bf16)
    weight_sum = jnp.sum(fifth[:, total:].astype(f32), axis=0).astype(bf16)
    sixth = exchange(
        jnp.concatenate(
            [summed.reshape(NM, NQ, CUT, width).transpose(1, 0, 2, 3), jnp.broadcast_to(weight_sum[None], (NQ, 2, CUT, width))], axis=1
        ),
        "zq",
    )
    sums = jnp.sum(sixth.astype(f32), axis=0).astype(bf16)
    last = exchange(
        jnp.concatenate([sums[:NM, None], jnp.broadcast_to(sums[None, NM:], (NM, 2, CUT, width))], axis=1), NEAR
    ).astype(f32)
    grad_features = last[:, 0].reshape(TILE, width)
    grad_weight = last[:, 1:].transpose(0, 2, 1, 3).reshape(TILE, 2 * width)
    return (hidden, grad_weight, grad_features)


def solution(mesh):
    parted = Mesh(mesh.devices.reshape(NY, NQ, NZP, NX, 2, 2), ROW + REP)
    in_specs = (
        P(ROW + REP, None),
        P(),
        P(ROW + REP, None),
        P(ROW, REP, None),
        P(ROW, REP),
        P(ROW, REP, None, None, None),
    )
    out_specs = (P(ROW + REP, None), P(), P(ROW + REP, None))
    return jax.shard_map(body, mesh=parted, in_specs=in_specs, out_specs=out_specs, check_vma=False)
```

```python
import jax
import jax.numpy as jnp
from jax import lax
from jax.experimental import pallas as pl
from jax.experimental.pallas import tpu as pltpu
from jax.sharding import Mesh, PartitionSpec as P

ROW = ("y", "zq", "zp", "xl")
REP = ("xh", "c")
NEAR = ("y", "zp", "xl")
NY, NQ, NZP, NX = 4, 8, 2, 2
NM = NY * NZP * NX
TILE = 128
CUT = TILE // NM


def exchange(array, axes):
    flat = array.reshape(array.shape[0], -1, array.shape[-1])
    return lax.all_to_all(flat, axes, split_axis=0, concat_axis=0, tiled=True).reshape(array.shape)


def add_up(terms):
    total = terms[0].astype(jnp.float32)
    for index in range(1, terms.shape[0]):
        total = total + terms[index].astype(jnp.float32)
    return total


def sum_kernel(parts_ref, out_ref):
    sums = parts_ref[0].astype(jnp.float32)
    for index in range(1, NQ):
        sums = sums + parts_ref[index].astype(jnp.float32)
    sums = sums.reshape(NM + 2, CUT, sums.shape[-1])
    shared = jnp.broadcast_to(sums[None, NM:], (NM, 2) + sums.shape[1:])
    packed = jnp.concatenate([sums[:NM, None], shared], axis=1)
    out_ref[...] = packed.reshape(out_ref.shape).astype(out_ref.dtype)


def unpack_kernel(parts_ref, weight_ref, features_ref):
    width = parts_ref.shape[-1]
    parts = parts_ref[...].astype(jnp.float32).reshape(NM, 3, CUT, width)
    features_ref[...] = parts[:, 0].reshape(TILE, width)
    weight_ref[:, :width] = parts[:, 1].reshape(TILE, width)
    weight_ref[:, width:] = parts[:, 2].reshape(TILE, width)


def body(features, weight, upstream, tile_owners, tile_counts, tile_values):
    f32, bf16 = jnp.float32, jnp.bfloat16
    width = features.shape[1]
    owners = tile_owners[:, 0, :]
    counts = tile_counts[:, 0]
    values = tile_values[:, 0]
    blocks, slots = owners.shape
    total = blocks * slots
    active = jnp.arange(slots, dtype=jnp.int32)[None, :] < counts[:, None]
    wide = exchange(jnp.broadcast_to(features[None], (NQ, TILE, width)), "zq")
    code = jnp.where(active, owners, -1).reshape(total).astype(bf16)
    code_rows = jnp.broadcast_to(jnp.pad(code, (0, width - total))[None, None, None, :], (NM, 1, CUT, width))
    halves = jnp.stack([upstream[:, :width], upstream[:, width:]])
    upstream_all = lax.all_gather(lax.all_gather(halves, "xh", axis=0), "c", axis=1)
    wide, code_rows, upstream_all = lax.optimization_barrier((wide, code_rows, upstream_all))

    slices = wide.reshape(NQ, NM, CUT, width).transpose(1, 0, 2, 3)
    second = exchange(jnp.concatenate([slices, code_rows], axis=1), NEAR)
    codes = second[:, NQ, 0, :total].astype(jnp.int32).reshape(NM * total)
    place = jnp.arange(NQ * NM, dtype=jnp.int32)
    member = place // NQ
    ident = (member // (NZP * NX)) * (NQ * NZP * NX) + (place % NQ) * (NZP * NX) + member % (NZP * NX)
    pick = (codes[:, None] == ident[None, :]).astype(bf16)
    table = second[:, :NQ].reshape(NQ * NM, CUT * width)
    wanted = jnp.dot(pick, table, preferred_element_type=f32).astype(bf16)
    third = exchange(wanted.reshape(NM, total, CUT, width), NEAR)
    picked = third.transpose(1, 0, 2, 3).reshape(blocks, slots, TILE, width)
    partial_value = jnp.einsum("btij,btjf->bif", values, picked, preferred_element_type=f32).astype(bf16)
    shared = lax.all_gather(partial_value, REP, axis=0)
    aggregated = add_up(shared).astype(bf16).reshape(blocks * TILE, width)
    upstream_all = upstream_all.transpose(0, 1, 3, 2, 4).reshape(blocks * TILE, 2 * width)

    pre_act = jnp.dot(aggregated, weight, preferred_element_type=f32)
    hidden_all, pullback = jax.vjp(jax.nn.gelu, pre_act)
    hidden = lax.dynamic_slice_in_dim(hidden_all.astype(bf16), lax.axis_index(REP) * TILE, TILE, 0)
    slope = pullback(upstream_all.astype(f32))[0].astype(bf16)
    weight_part = jnp.dot(aggregated.T, slope, preferred_element_type=f32)
    back_rows = jnp.dot(slope, weight.T, preferred_element_type=f32).astype(bf16).reshape(blocks, TILE, width)
    parts = jnp.einsum("btji,bjf->btif", values, back_rows, preferred_element_type=f32).astype(bf16)

    parts = parts.reshape(total, NM, CUT, width).transpose(1, 0, 2, 3)
    weight_cut = weight_part.astype(bf16).reshape(NM, CUT, 2, width).transpose(0, 2, 1, 3)
    fifth = exchange(jnp.concatenate([parts, weight_cut], axis=1), NEAR)
    summed = jnp.dot(pick.T, fifth[:, :total].reshape(NM * total, CUT * width), preferred_element_type=f32).astype(bf16)
    weight_sum = add_up(fifth[:, total:]).astype(bf16)
    sixth = exchange(
        jnp.concatenate(
            [
                summed.reshape(NM, NQ, CUT, width).transpose(1, 0, 2, 3),
                jnp.broadcast_to(weight_sum[None], (NQ, 2, CUT, width)),
            ],
            axis=1,
        ).reshape(NQ, (NM + 2) * CUT, width),
        "zq",
    )
    near = pl.BlockSpec(memory_space=pltpu.VMEM)
    room = pltpu.CompilerParams(vmem_limit_bytes=4 * 1024 * 1024)
    packed = pl.pallas_call(
        sum_kernel,
        out_shape=jax.ShapeDtypeStruct((NM, 3 * CUT, width), bf16),
        in_specs=[near],
        out_specs=near,
        compiler_params=room,
        name="sum_far",
    )(sixth)
    last = exchange(packed, NEAR)
    grad_weight, grad_features = pl.pallas_call(
        unpack_kernel,
        out_shape=(jax.ShapeDtypeStruct((TILE, 2 * width), f32), jax.ShapeDtypeStruct((TILE, width), f32)),
        in_specs=[near],
        out_specs=(near, near),
        compiler_params=room,
        name="unpack",
    )(last)
    return (hidden, grad_weight, grad_features)


def solution(mesh):
    parted = Mesh(mesh.devices.reshape(NY, NQ, NZP, NX, 2, 2), ROW + REP)
    in_specs = (
        P(ROW + REP, None),
        P(),
        P(ROW + REP, None),
        P(ROW, REP, None),
        P(ROW, REP),
        P(ROW, REP, None, None, None),
    )
    out_specs = (P(ROW + REP, None), P(), P(ROW + REP, None))
    return jax.shard_map(body, mesh=parted, in_specs=in_specs, out_specs=out_specs, check_vma=False)
```

```python
import jax
import jax.numpy as jnp
from jax import lax
from jax.experimental import pallas as pl
from jax.experimental.pallas import tpu as pltpu
from jax.sharding import Mesh, PartitionSpec as P

ROW = ("y", "zq", "zp", "xl")
REP = ("xh", "c")
NEAR = ("y", "zp", "xl")
NY, NQ, NZP, NX = 4, 8, 2, 2
NM = NY * NZP * NX
TILE = 128
CUT = TILE // NM


def exchange(array, axes):
    flat = array.reshape(array.shape[0], -1, array.shape[-1])
    return lax.all_to_all(flat, axes, split_axis=0, concat_axis=0, tiled=True).reshape(array.shape)


def add_up(terms):
    total = terms[0].astype(jnp.float32)
    for index in range(1, terms.shape[0]):
        total = total + terms[index].astype(jnp.float32)
    return total


def start_kernel(features_ref, owners_ref, counts_ref, out_ref):
    width = features_ref.shape[1]
    blocks, slots = owners_ref.shape
    lane = lax.broadcasted_iota(jnp.int32, (CUT, width), 1)
    code = jnp.full((CUT, width), -1, jnp.int32)
    for block in range(blocks):
        for slot in range(slots):
            wanted = jnp.where(slot < counts_ref[0, block], owners_ref[block, slot], -1)
            code = jnp.where(lane == block * slots + slot, wanted, code)
    code = jnp.broadcast_to(code.astype(jnp.float32)[None], (NM, CUT, width))
    cut = features_ref[...].astype(jnp.float32).reshape(NM, CUT, width)
    out_ref[...] = jnp.concatenate([cut, code], axis=1).astype(out_ref.dtype)


def sum_kernel(parts_ref, out_ref):
    sums = parts_ref[0].astype(jnp.float32)
    for index in range(1, NQ):
        sums = sums + parts_ref[index].astype(jnp.float32)
    sums = sums.reshape(NM + 2, CUT, sums.shape[-1])
    shared = jnp.broadcast_to(sums[None, NM:], (NM, 2) + sums.shape[1:])
    packed = jnp.concatenate([sums[:NM, None], shared], axis=1)
    out_ref[...] = packed.reshape(out_ref.shape).astype(out_ref.dtype)


def unpack_kernel(parts_ref, weight_ref, features_ref):
    width = parts_ref.shape[-1]
    parts = parts_ref[...].astype(jnp.float32).reshape(NM, 3, CUT, width)
    features_ref[...] = parts[:, 0].reshape(TILE, width)
    weight_ref[:, :width] = parts[:, 1].reshape(TILE, width)
    weight_ref[:, width:] = parts[:, 2].reshape(TILE, width)


def body(features, weight, upstream, tile_owners, tile_counts, tile_values):
    f32, bf16 = jnp.float32, jnp.bfloat16
    width = features.shape[1]
    values = tile_values[:, 0]
    blocks, slots = values.shape[:2]
    total = blocks * slots
    near = pl.BlockSpec(memory_space=pltpu.VMEM)
    scalar = pl.BlockSpec(memory_space=pltpu.SMEM)
    room = pltpu.CompilerParams(vmem_limit_bytes=4 * 1024 * 1024)

    start = pl.pallas_call(
        start_kernel,
        out_shape=jax.ShapeDtypeStruct((NM, 2 * CUT, width), bf16),
        in_specs=[near, scalar, scalar],
        out_specs=near,
        compiler_params=room,
        name="start",
    )(features, tile_owners.reshape(blocks, slots), tile_counts.reshape(1, blocks))
    first = exchange(start, NEAR)
    spread = jnp.broadcast_to(first[None, :, :CUT], (NQ, NM, CUT, width)).reshape(NQ, NM * CUT, width)
    table = exchange(spread, "zq")
    codes = first[:, CUT, :total].astype(jnp.int32).reshape(NM * total)
    place = jnp.arange(NQ * NM, dtype=jnp.int32)
    ident = ((place // (NZP * NX)) % NY) * (NQ * NZP * NX) + (place // NM) * (NZP * NX) + place % (NZP * NX)
    pick = (codes[:, None] == ident[None, :]).astype(bf16)
    halves = jnp.stack([upstream[:, :width], upstream[:, width:]])
    first, halves = lax.optimization_barrier((first, halves))
    upstream_all = lax.all_gather(lax.all_gather(halves, "xh", axis=0), "c", axis=1)
    table, upstream_all, pick = lax.optimization_barrier((table, upstream_all, pick))
    table = table.reshape(NQ * NM, CUT * width)
    wanted = jnp.dot(pick, table, preferred_element_type=f32).astype(bf16)
    third = exchange(wanted.reshape(NM, total, CUT, width), NEAR)
    picked = third.transpose(1, 0, 2, 3).reshape(blocks, slots, TILE, width)
    partial_value = jnp.einsum("btij,btjf->bif", values, picked, preferred_element_type=f32).astype(bf16)
    shared = lax.all_gather(partial_value, REP, axis=0)
    aggregated = add_up(shared).astype(bf16).reshape(blocks * TILE, width)
    upstream_all = upstream_all.transpose(0, 1, 3, 2, 4).reshape(blocks * TILE, 2 * width)

    pre_act = jnp.dot(aggregated, weight, preferred_element_type=f32)
    hidden_all, pullback = jax.vjp(jax.nn.gelu, pre_act)
    hidden = lax.dynamic_slice_in_dim(hidden_all.astype(bf16), lax.axis_index(REP) * TILE, TILE, 0)
    slope = pullback(upstream_all.astype(f32))[0].astype(bf16)
    weight_part = jnp.dot(aggregated.T, slope, preferred_element_type=f32)
    back_rows = jnp.dot(slope, weight.T, preferred_element_type=f32).astype(bf16).reshape(blocks, TILE, width)
    parts = jnp.einsum("btji,bjf->btif", values, back_rows, preferred_element_type=f32).astype(bf16)

    parts = parts.reshape(total, NM, CUT, width).transpose(1, 0, 2, 3)
    weight_cut = weight_part.astype(bf16).reshape(NM, CUT, 2, width).transpose(0, 2, 1, 3)
    fifth = exchange(jnp.concatenate([parts, weight_cut], axis=1), NEAR)
    summed = jnp.dot(pick.T, fifth[:, :total].reshape(NM * total, CUT * width), preferred_element_type=f32).astype(bf16)
    weight_sum = add_up(fifth[:, total:]).astype(bf16)
    sixth = exchange(
        jnp.concatenate(
            [
                summed.reshape(NQ, NM, CUT, width),
                jnp.broadcast_to(weight_sum[None], (NQ, 2, CUT, width)),
            ],
            axis=1,
        ).reshape(NQ, (NM + 2) * CUT, width),
        "zq",
    )
    packed = pl.pallas_call(
        sum_kernel,
        out_shape=jax.ShapeDtypeStruct((NM, 3 * CUT, width), bf16),
        in_specs=[near],
        out_specs=near,
        compiler_params=room,
        name="sum_far",
    )(sixth)
    last = exchange(packed, NEAR)
    grad_weight, grad_features = pl.pallas_call(
        unpack_kernel,
        out_shape=(jax.ShapeDtypeStruct((TILE, 2 * width), f32), jax.ShapeDtypeStruct((TILE, width), f32)),
        in_specs=[near],
        out_specs=(near, near),
        compiler_params=room,
        name="unpack",
    )(last)
    return (hidden, grad_weight, grad_features)


def solution(mesh):
    parted = Mesh(mesh.devices.reshape(NY, NQ, NZP, NX, 2, 2), ROW + REP)
    in_specs = (
        P(ROW + REP, None),
        P(),
        P(ROW + REP, None),
        P(ROW, REP, None),
        P(ROW, REP),
        P(ROW, REP, None, None, None),
    )
    out_specs = (P(ROW + REP, None), P(), P(ROW + REP, None))
    return jax.shard_map(body, mesh=parted, in_specs=in_specs, out_specs=out_specs, check_vma=False)
```

```python
import jax
import jax.numpy as jnp
from jax import lax
from jax.experimental import pallas as pl
from jax.experimental.pallas import tpu as pltpu
from jax.sharding import Mesh, PartitionSpec as P

ROW = ("y", "zq", "zp", "xl")
REP = ("xh", "c")
NEAR = ("y", "zp", "xl")
NY, NQ, NZP, NX = 4, 8, 2, 2
NM = NY * NZP * NX
TILE = 128
CUT = TILE // NM


ORDER = [(index + NQ // 2) % NQ for index in range(NQ)]


def exchange(array, axes, groups=None):
    flat = array.reshape(array.shape[0], -1, array.shape[-1])
    flat = lax.all_to_all(flat, axes, split_axis=0, concat_axis=0, axis_index_groups=groups, tiled=True)
    return flat.reshape(array.shape)


def add_up(terms):
    total = terms[0].astype(jnp.float32)
    for index in range(1, terms.shape[0]):
        total = total + terms[index].astype(jnp.float32)
    return total


def start_kernel(features_ref, owners_ref, counts_ref, out_ref):
    width = features_ref.shape[1]
    blocks, slots = owners_ref.shape
    lane = lax.broadcasted_iota(jnp.int32, (CUT, width), 1)
    code = jnp.full((CUT, width), -1, jnp.int32)
    for block in range(blocks):
        for slot in range(slots):
            wanted = jnp.where(slot < counts_ref[0, block], owners_ref[block, slot], -1)
            code = jnp.where(lane == block * slots + slot, wanted, code)
    code = jnp.broadcast_to(code.astype(jnp.float32)[None], (NM, CUT, width))
    cut = features_ref[...].astype(jnp.float32).reshape(NM, CUT, width)
    out_ref[...] = jnp.concatenate([cut, code], axis=1).astype(out_ref.dtype)


def sum_kernel(parts_ref, out_ref):
    sums = parts_ref[0].astype(jnp.float32)
    for index in range(1, NQ):
        sums = sums + parts_ref[index].astype(jnp.float32)
    sums = sums.reshape(NM + 2, CUT, sums.shape[-1])
    shared = jnp.broadcast_to(sums[None, NM:], (NM, 2) + sums.shape[1:])
    packed = jnp.concatenate([sums[:NM, None], shared], axis=1)
    out_ref[...] = packed.reshape(out_ref.shape).astype(out_ref.dtype)


def unpack_kernel(parts_ref, weight_ref, features_ref):
    width = parts_ref.shape[-1]
    parts = parts_ref[...].astype(jnp.float32).reshape(NM, 3, CUT, width)
    features_ref[...] = parts[:, 0].reshape(TILE, width)
    weight_ref[:, :width] = parts[:, 1].reshape(TILE, width)
    weight_ref[:, width:] = parts[:, 2].reshape(TILE, width)


def body(features, weight, upstream, tile_owners, tile_counts, tile_values):
    f32, bf16 = jnp.float32, jnp.bfloat16
    width = features.shape[1]
    values = tile_values[:, 0]
    blocks, slots = values.shape[:2]
    total = blocks * slots
    near = pl.BlockSpec(memory_space=pltpu.VMEM)
    scalar = pl.BlockSpec(memory_space=pltpu.SMEM)
    room = pltpu.CompilerParams(vmem_limit_bytes=4 * 1024 * 1024)

    start = pl.pallas_call(
        start_kernel,
        out_shape=jax.ShapeDtypeStruct((NM, 2 * CUT, width), bf16),
        in_specs=[near, scalar, scalar],
        out_specs=near,
        compiler_params=room,
        name="start",
    )(features, tile_owners.reshape(blocks, slots), tile_counts.reshape(1, blocks))
    first = exchange(start, NEAR)
    spread = jnp.broadcast_to(first[None, :, :CUT], (NQ, NM, CUT, width)).reshape(NQ, NM * CUT, width)
    table = exchange(spread, "zq", [ORDER])
    codes = first[:, CUT, :total].astype(jnp.int32).reshape(NM * total)
    place = jnp.arange(NQ * NM, dtype=jnp.int32)
    ident = ((place // (NZP * NX)) % NY) * (NQ * NZP * NX) + ((place // NM + NQ // 2) % NQ) * (NZP * NX) + place % (NZP * NX)
    pick = (codes[:, None] == ident[None, :]).astype(bf16)
    halves = jnp.stack([upstream[:, :width], upstream[:, width:]])
    first, halves = lax.optimization_barrier((first, halves))
    upstream_all = lax.all_gather(lax.all_gather(halves, "xh", axis=0), "c", axis=1)
    table, upstream_all, pick = lax.optimization_barrier((table, upstream_all, pick))
    table = table.reshape(NQ * NM, CUT * width)
    wanted = jnp.dot(pick, table, preferred_element_type=f32).astype(bf16)
    third = exchange(wanted.reshape(NM, total, CUT, width), NEAR)
    picked = third.transpose(1, 0, 2, 3).reshape(blocks, slots, TILE, width)
    partial_value = jnp.einsum("btij,btjf->bif", values, picked, preferred_element_type=f32).astype(bf16)
    shared = lax.all_gather(partial_value, REP, axis=0)
    aggregated = add_up(shared).astype(bf16).reshape(blocks * TILE, width)
    upstream_all = upstream_all.transpose(0, 1, 3, 2, 4).reshape(blocks * TILE, 2 * width)

    pre_act = jnp.dot(aggregated, weight, preferred_element_type=f32)
    hidden_all, pullback = jax.vjp(jax.nn.gelu, pre_act)
    hidden = lax.dynamic_slice_in_dim(hidden_all.astype(bf16), lax.axis_index(REP) * TILE, TILE, 0)
    slope = pullback(upstream_all.astype(f32))[0].astype(bf16)
    weight_part = jnp.dot(aggregated.T, slope, preferred_element_type=f32)
    back_rows = jnp.dot(slope, weight.T, preferred_element_type=f32).astype(bf16).reshape(blocks, TILE, width)
    parts = jnp.einsum("btji,bjf->btif", values, back_rows, preferred_element_type=f32).astype(bf16)

    parts = parts.reshape(total, NM, CUT, width).transpose(1, 0, 2, 3)
    weight_cut = weight_part.astype(bf16).reshape(NM, CUT, 2, width).transpose(0, 2, 1, 3)
    fifth = exchange(jnp.concatenate([parts, weight_cut], axis=1), NEAR)
    summed = jnp.dot(pick.T, fifth[:, :total].reshape(NM * total, CUT * width), preferred_element_type=f32).astype(bf16)
    weight_sum = add_up(fifth[:, total:]).astype(bf16)
    sixth = exchange(
        jnp.concatenate(
            [
                summed.reshape(NQ, NM, CUT, width),
                jnp.broadcast_to(weight_sum[None], (NQ, 2, CUT, width)),
            ],
            axis=1,
        ).reshape(NQ, (NM + 2) * CUT, width),
        "zq",
        [ORDER],
    )
    packed = pl.pallas_call(
        sum_kernel,
        out_shape=jax.ShapeDtypeStruct((NM, 3 * CUT, width), bf16),
        in_specs=[near],
        out_specs=near,
        compiler_params=room,
        name="sum_far",
    )(sixth)
    last = exchange(packed, NEAR)
    grad_weight, grad_features = pl.pallas_call(
        unpack_kernel,
        out_shape=(jax.ShapeDtypeStruct((TILE, 2 * width), f32), jax.ShapeDtypeStruct((TILE, width), f32)),
        in_specs=[near],
        out_specs=(near, near),
        compiler_params=room,
        name="unpack",
    )(last)
    return (hidden, grad_weight, grad_features)


def solution(mesh):
    parted = Mesh(mesh.devices.reshape(NY, NQ, NZP, NX, 2, 2), ROW + REP)
    in_specs = (
        P(ROW + REP, None),
        P(),
        P(ROW + REP, None),
        P(ROW, REP, None),
        P(ROW, REP),
        P(ROW, REP, None, None, None),
    )
    out_specs = (P(ROW + REP, None), P(), P(ROW + REP, None))
    return jax.shard_map(body, mesh=parted, in_specs=in_specs, out_specs=out_specs, check_vma=False)
```

```python
import jax
import jax.numpy as jnp
from jax import lax
from jax.experimental import pallas as pl
from jax.experimental.pallas import tpu as pltpu
from jax.sharding import Mesh, PartitionSpec as P

ROW = ("y", "zq", "zp", "xl")
REP = ("xh", "c")
NEAR = ("y", "zp", "xl")
NY, NQ, NZP, NX = 4, 8, 2, 2
NM = NY * NZP * NX
TILE = 128
CUT = TILE // NM


AHEAD, BACK = 5, 4


def order(lead):
    return [[(index + lead) % NQ for index in range(NQ)]]


def rows_in(lead):
    place = jnp.arange(NQ * NM, dtype=jnp.int32)
    zq = (place // NM + lead) % NQ
    return ((place // (NZP * NX)) % NY) * (NQ * NZP * NX) + zq * (NZP * NX) + place % (NZP * NX)


def exchange(array, axes, groups=None):
    flat = array.reshape(array.shape[0], -1, array.shape[-1])
    flat = lax.all_to_all(flat, axes, split_axis=0, concat_axis=0, axis_index_groups=groups, tiled=True)
    return flat.reshape(array.shape)


def add_up(terms):
    total = terms[0].astype(jnp.float32)
    for index in range(1, terms.shape[0]):
        total = total + terms[index].astype(jnp.float32)
    return total


def start_kernel(features_ref, owners_ref, counts_ref, out_ref):
    width = features_ref.shape[1]
    blocks, slots = owners_ref.shape
    lane = lax.broadcasted_iota(jnp.int32, (CUT, width), 1)
    code = jnp.full((CUT, width), -1, jnp.int32)
    for block in range(blocks):
        for slot in range(slots):
            wanted = jnp.where(slot < counts_ref[0, block], owners_ref[block, slot], -1)
            code = jnp.where(lane == block * slots + slot, wanted, code)
    code = jnp.broadcast_to(code.astype(jnp.float32)[None], (NM, CUT, width))
    cut = features_ref[...].astype(jnp.float32).reshape(NM, CUT, width)
    out_ref[...] = jnp.concatenate([cut, code], axis=1).astype(out_ref.dtype)


def sum_kernel(parts_ref, out_ref):
    sums = parts_ref[0].astype(jnp.float32)
    for index in range(1, NQ):
        sums = sums + parts_ref[index].astype(jnp.float32)
    sums = sums.reshape(NM + 2, CUT, sums.shape[-1])
    shared = jnp.broadcast_to(sums[None, NM:], (NM, 2) + sums.shape[1:])
    packed = jnp.concatenate([sums[:NM, None], shared], axis=1)
    out_ref[...] = packed.reshape(out_ref.shape).astype(out_ref.dtype)


def unpack_kernel(parts_ref, weight_ref, features_ref):
    width = parts_ref.shape[-1]
    parts = parts_ref[...].astype(jnp.float32).reshape(NM, 3, CUT, width)
    features_ref[...] = parts[:, 0].reshape(TILE, width)
    weight_ref[:, :width] = parts[:, 1].reshape(TILE, width)
    weight_ref[:, width:] = parts[:, 2].reshape(TILE, width)


def body(features, weight, upstream, tile_owners, tile_counts, tile_values):
    f32, bf16 = jnp.float32, jnp.bfloat16
    width = features.shape[1]
    values = tile_values[:, 0]
    blocks, slots = values.shape[:2]
    total = blocks * slots
    near = pl.BlockSpec(memory_space=pltpu.VMEM)
    scalar = pl.BlockSpec(memory_space=pltpu.SMEM)
    room = pltpu.CompilerParams(vmem_limit_bytes=4 * 1024 * 1024)

    start = pl.pallas_call(
        start_kernel,
        out_shape=jax.ShapeDtypeStruct((NM, 2 * CUT, width), bf16),
        in_specs=[near, scalar, scalar],
        out_specs=near,
        compiler_params=room,
        name="start",
    )(features, tile_owners.reshape(blocks, slots), tile_counts.reshape(1, blocks))
    first = exchange(start, NEAR)
    spread = jnp.broadcast_to(first[None, :, :CUT], (NQ, NM, CUT, width)).reshape(NQ, NM * CUT, width)
    table = exchange(spread, "zq", order(AHEAD))
    codes = first[:, CUT, :total].astype(jnp.int32).reshape(NM * total)
    choose = (codes[:, None] == rows_in(AHEAD)[None, :]).astype(bf16)
    pick = (codes[:, None] == rows_in(BACK)[None, :]).astype(bf16)
    halves = jnp.stack([upstream[:, :width], upstream[:, width:]])
    first, halves = lax.optimization_barrier((first, halves))
    upstream_all = lax.all_gather(lax.all_gather(halves, "xh", axis=0), "c", axis=1)
    table, upstream_all, choose, pick = lax.optimization_barrier((table, upstream_all, choose, pick))
    table = table.reshape(NQ * NM, CUT * width)
    wanted = jnp.dot(choose, table, preferred_element_type=f32).astype(bf16)
    third = exchange(wanted.reshape(NM, total, CUT, width), NEAR)
    picked = third.transpose(1, 0, 2, 3).reshape(blocks, slots, TILE, width)
    partial_value = jnp.einsum("btij,btjf->bif", values, picked, preferred_element_type=f32).astype(bf16)
    shared = lax.all_gather(partial_value, REP, axis=0)
    aggregated = add_up(shared).astype(bf16).reshape(blocks * TILE, width)
    upstream_all = upstream_all.transpose(0, 1, 3, 2, 4).reshape(blocks * TILE, 2 * width)

    pre_act = jnp.dot(aggregated, weight, preferred_element_type=f32)
    hidden_all, pullback = jax.vjp(jax.nn.gelu, pre_act)
    hidden = lax.dynamic_slice_in_dim(hidden_all.astype(bf16), lax.axis_index(REP) * TILE, TILE, 0)
    slope = pullback(upstream_all.astype(f32))[0].astype(bf16)
    weight_part = jnp.dot(aggregated.T, slope, preferred_element_type=f32)
    back_rows = jnp.dot(slope, weight.T, preferred_element_type=f32).astype(bf16).reshape(blocks, TILE, width)
    parts = jnp.einsum("btji,bjf->btif", values, back_rows, preferred_element_type=f32).astype(bf16)

    parts = parts.reshape(total, NM, CUT, width).transpose(1, 0, 2, 3)
    weight_cut = weight_part.astype(bf16).reshape(NM, CUT, 2, width).transpose(0, 2, 1, 3)
    fifth = exchange(jnp.concatenate([parts, weight_cut], axis=1), NEAR)
    summed = jnp.dot(pick.T, fifth[:, :total].reshape(NM * total, CUT * width), preferred_element_type=f32).astype(bf16)
    weight_sum = add_up(fifth[:, total:]).astype(bf16)
    sixth = exchange(
        jnp.concatenate(
            [
                summed.reshape(NQ, NM, CUT, width),
                jnp.broadcast_to(weight_sum[None], (NQ, 2, CUT, width)),
            ],
            axis=1,
        ).reshape(NQ, (NM + 2) * CUT, width),
        "zq",
        order(BACK),
    )
    packed = pl.pallas_call(
        sum_kernel,
        out_shape=jax.ShapeDtypeStruct((NM, 3 * CUT, width), bf16),
        in_specs=[near],
        out_specs=near,
        compiler_params=room,
        name="sum_far",
    )(sixth)
    last = exchange(packed, NEAR)
    grad_weight, grad_features = pl.pallas_call(
        unpack_kernel,
        out_shape=(jax.ShapeDtypeStruct((TILE, 2 * width), f32), jax.ShapeDtypeStruct((TILE, width), f32)),
        in_specs=[near],
        out_specs=(near, near),
        compiler_params=room,
        name="unpack",
    )(last)
    return (hidden, grad_weight, grad_features)


def solution(mesh):
    parted = Mesh(mesh.devices.reshape(NY, NQ, NZP, NX, 2, 2), ROW + REP)
    in_specs = (
        P(ROW + REP, None),
        P(),
        P(ROW + REP, None),
        P(ROW, REP, None),
        P(ROW, REP),
        P(ROW, REP, None, None, None),
    )
    out_specs = (P(ROW + REP, None), P(), P(ROW + REP, None))
    return jax.shard_map(body, mesh=parted, in_specs=in_specs, out_specs=out_specs, check_vma=False)
```

```python
import jax
import jax.numpy as jnp
from jax import lax
from jax.experimental import pallas as pl
from jax.experimental.pallas import tpu as pltpu
from jax.sharding import Mesh, PartitionSpec as P

ROW = ("y", "zq", "zp", "xl")
REP = ("xh", "c")
NEAR = ("y", "zp", "xl")
NY, NQ, NZP, NX = 4, 8, 2, 2
NM = NY * NZP * NX
TILE = 128
CUT = TILE // NM


AHEAD, BACK = 5, 4


def order(lead):
    return [[(index + lead) % NQ for index in range(NQ)]]


def swap(array):
    return jnp.concatenate([array[NM // 2 :], array[: NM // 2]])


def rows_in(lead):
    place = jnp.arange(NQ * NM, dtype=jnp.int32)
    zq = (place // NM + lead) % NQ
    return ((place // (NZP * NX)) % NY) * (NQ * NZP * NX) + zq * (NZP * NX) + place % (NZP * NX)


def exchange(array, axes, groups=None):
    flat = array.reshape(array.shape[0], -1, array.shape[-1])
    flat = lax.all_to_all(flat, axes, split_axis=0, concat_axis=0, axis_index_groups=groups, tiled=True)
    return flat.reshape(array.shape)


def add_up(terms):
    total = terms[0].astype(jnp.float32)
    for index in range(1, terms.shape[0]):
        total = total + terms[index].astype(jnp.float32)
    return total


def start_kernel(features_in, owners_in, counts_in, out_ref, features_ref, owners_ref, counts_ref, done):
    copies = [
        pltpu.make_async_copy(owners_in, owners_ref, done.at[0]),
        pltpu.make_async_copy(counts_in, counts_ref, done.at[1]),
        pltpu.make_async_copy(features_in, features_ref, done.at[2]),
    ]
    for copy in copies:
        copy.start()
    for copy in copies:
        copy.wait()
    width = features_ref.shape[1]
    blocks, slots = owners_ref.shape
    lane = lax.broadcasted_iota(jnp.int32, (CUT, width), 1)
    code = jnp.full((CUT, width), -1, jnp.int32)
    for block in range(blocks):
        for slot in range(slots):
            wanted = jnp.where(slot < counts_ref[0, block], owners_ref[block, slot], -1)
            code = jnp.where(lane == block * slots + slot, wanted, code)
    code = jnp.broadcast_to(code.astype(jnp.float32)[None], (NM, CUT, width))
    cut = swap(features_ref[...].astype(jnp.float32).reshape(NM, CUT, width))
    out_ref[...] = jnp.concatenate([cut, code], axis=1).astype(out_ref.dtype)


def sum_kernel(parts_ref, out_ref):
    sums = parts_ref[0].astype(jnp.float32)
    for index in range(1, NQ):
        sums = sums + parts_ref[index].astype(jnp.float32)
    sums = sums.reshape(NM + 2, CUT, sums.shape[-1])
    shared = jnp.broadcast_to(sums[None, NM:], (NM, 2) + sums.shape[1:])
    packed = jnp.concatenate([sums[:NM, None], shared], axis=1)
    out_ref[...] = packed.reshape(out_ref.shape).astype(out_ref.dtype)


def unpack_kernel(parts_ref, weight_ref, features_ref):
    width = parts_ref.shape[-1]
    parts = parts_ref[...].astype(jnp.float32).reshape(NM, 3, CUT, width)
    features_ref[...] = parts[:, 0].reshape(TILE, width)
    weight_ref[:, :width] = parts[:, 1].reshape(TILE, width)
    weight_ref[:, width:] = parts[:, 2].reshape(TILE, width)


def body(features, weight, upstream, tile_owners, tile_counts, tile_values):
    f32, bf16 = jnp.float32, jnp.bfloat16
    width = features.shape[1]
    values = tile_values[:, 0]
    blocks, slots = values.shape[:2]
    total = blocks * slots
    near = pl.BlockSpec(memory_space=pltpu.VMEM)
    scalar = pl.BlockSpec(memory_space=pltpu.SMEM)
    room = pltpu.CompilerParams(vmem_limit_bytes=4 * 1024 * 1024)

    start = pl.pallas_call(
        start_kernel,
        out_shape=jax.ShapeDtypeStruct((NM, 2 * CUT, width), bf16),
        in_specs=[pl.BlockSpec(memory_space=pl.ANY)] * 3,
        scratch_shapes=[
            pltpu.VMEM((TILE, width), bf16),
            pltpu.SMEM((blocks, slots), jnp.int32),
            pltpu.SMEM((1, blocks), jnp.int32),
            pltpu.SemaphoreType.DMA((3,)),
        ],
        name="start",
    )(features, tile_owners.reshape(blocks, slots), tile_counts.reshape(1, blocks))
    first = swap(exchange(start, NEAR, [[index ^ (NM // 2) for index in range(NM)]]))
    spread = jnp.broadcast_to(first[None, :, :CUT], (NQ, NM, CUT, width)).reshape(NQ, NM * CUT, width)
    table = exchange(spread, "zq", order(AHEAD))
    codes = first[:, CUT, :total].astype(jnp.int32).reshape(NM * total)
    choose = (codes[:, None] == rows_in(AHEAD)[None, :]).astype(bf16)
    pick = (codes[:, None] == rows_in(BACK)[None, :]).astype(bf16)
    halves = jnp.stack([upstream[:, :width], upstream[:, width:]])
    first, halves = lax.optimization_barrier((first, halves))
    upstream_all = lax.all_gather(lax.all_gather(halves, "xh", axis=0), "c", axis=1)
    table, upstream_all, choose, pick = lax.optimization_barrier((table, upstream_all, choose, pick))
    table = table.reshape(NQ * NM, CUT * width)
    wanted = jnp.dot(choose, table, preferred_element_type=f32).astype(bf16)
    third = exchange(wanted.reshape(NM, total, CUT, width), NEAR)
    picked = third.transpose(1, 0, 2, 3).reshape(blocks, slots, TILE, width)
    partial_value = jnp.einsum("btij,btjf->bif", values, picked, preferred_element_type=f32).astype(bf16)
    shared = lax.all_gather(partial_value, REP, axis=0)
    aggregated = add_up(shared).astype(bf16).reshape(blocks * TILE, width)
    upstream_all = upstream_all.transpose(0, 1, 3, 2, 4).reshape(blocks * TILE, 2 * width)

    pre_act = jnp.dot(aggregated, weight, preferred_element_type=f32)
    hidden_all, pullback = jax.vjp(jax.nn.gelu, pre_act)
    hidden = lax.dynamic_slice_in_dim(hidden_all.astype(bf16), lax.axis_index(REP) * TILE, TILE, 0)
    slope = pullback(upstream_all.astype(f32))[0].astype(bf16)
    weight_part = jnp.dot(aggregated.T, slope, preferred_element_type=f32)
    back_rows = jnp.dot(slope, weight.T, preferred_element_type=f32).astype(bf16).reshape(blocks, TILE, width)
    parts = jnp.einsum("btji,bjf->btif", values, back_rows, preferred_element_type=f32).astype(bf16)

    parts = parts.reshape(total, NM, CUT, width).transpose(1, 0, 2, 3)
    weight_cut = weight_part.astype(bf16).reshape(NM, CUT, 2, width).transpose(0, 2, 1, 3)
    fifth = exchange(jnp.concatenate([parts, weight_cut], axis=1), NEAR)
    summed = jnp.dot(pick.T, fifth[:, :total].reshape(NM * total, CUT * width), preferred_element_type=f32).astype(bf16)
    weight_sum = add_up(fifth[:, total:]).astype(bf16)
    sixth = exchange(
        jnp.concatenate(
            [
                summed.reshape(NQ, NM, CUT, width),
                jnp.broadcast_to(weight_sum[None], (NQ, 2, CUT, width)),
            ],
            axis=1,
        ).reshape(NQ, (NM + 2) * CUT, width),
        "zq",
        order(BACK),
    )
    packed = pl.pallas_call(
        sum_kernel,
        out_shape=jax.ShapeDtypeStruct((NM, 3 * CUT, width), bf16),
        in_specs=[near],
        out_specs=near,
        compiler_params=room,
        name="sum_far",
    )(sixth)
    last = exchange(packed, NEAR)
    grad_weight, grad_features = pl.pallas_call(
        unpack_kernel,
        out_shape=(jax.ShapeDtypeStruct((TILE, 2 * width), f32), jax.ShapeDtypeStruct((TILE, width), f32)),
        in_specs=[near],
        out_specs=(near, near),
        compiler_params=room,
        name="unpack",
    )(last)
    return (hidden, grad_weight, grad_features)


def solution(mesh):
    parted = Mesh(mesh.devices.reshape(NY, NQ, NZP, NX, 2, 2), ROW + REP)
    in_specs = (
        P(ROW + REP, None),
        P(),
        P(ROW + REP, None),
        P(ROW, REP, None),
        P(ROW, REP),
        P(ROW, REP, None, None, None),
    )
    out_specs = (P(ROW + REP, None), P(), P(ROW + REP, None))
    return jax.shard_map(body, mesh=parted, in_specs=in_specs, out_specs=out_specs, check_vma=False)
```

```python
import jax
import jax.numpy as jnp
from jax import lax
from jax.experimental import pallas as pl
from jax.experimental.pallas import tpu as pltpu
from jax.sharding import Mesh, PartitionSpec as P

ROW = ("y", "zq", "zp", "xl")
REP = ("xh", "c")
NEAR = ("y", "zp", "xl")
NY, NQ, NZP, NX = 4, 8, 2, 2
NM = NY * NZP * NX
TILE = 128
CUT = TILE // NM


AHEAD, BACK = 5, 4


def order(lead):
    return [[(index + lead) % NQ for index in range(NQ)]]


def swap(array):
    return jnp.concatenate([array[NM // 2 :], array[: NM // 2]])


def rows_in(lead):
    place = jnp.arange(NQ * NM, dtype=jnp.int32)
    zq = (place // NM + lead) % NQ
    return ((place // (NZP * NX)) % NY) * (NQ * NZP * NX) + zq * (NZP * NX) + place % (NZP * NX)


def exchange(array, axes, groups=None):
    flat = array.reshape(array.shape[0], -1, array.shape[-1])
    flat = lax.all_to_all(flat, axes, split_axis=0, concat_axis=0, axis_index_groups=groups, tiled=True)
    return flat.reshape(array.shape)


def add_up(terms):
    total = terms[0].astype(jnp.float32)
    for index in range(1, terms.shape[0]):
        total = total + terms[index].astype(jnp.float32)
    return total


def start_kernel(features_in, owners_in, counts_in, out_ref, features_ref, owners_ref, counts_ref, done):
    copies = [
        pltpu.make_async_copy(owners_in, owners_ref, done.at[0]),
        pltpu.make_async_copy(counts_in, counts_ref, done.at[1]),
        pltpu.make_async_copy(features_in, features_ref, done.at[2]),
    ]
    for copy in copies:
        copy.start()
    for copy in copies:
        copy.wait()
    width = features_ref.shape[1]
    blocks, slots = owners_ref.shape
    lane = lax.broadcasted_iota(jnp.int32, (CUT, width), 1)
    code = jnp.full((CUT, width), -1, jnp.int32)
    for block in range(blocks):
        for slot in range(slots):
            wanted = jnp.where(slot < counts_ref[0, block], owners_ref[block, slot], -1)
            code = jnp.where(lane == block * slots + slot, wanted, code)
    code = jnp.broadcast_to(code.astype(jnp.float32)[None], (NM, CUT, width))
    cut = swap(features_ref[...].astype(jnp.float32).reshape(NM, CUT, width))
    out_ref[...] = jnp.concatenate([cut, code], axis=1).astype(out_ref.dtype)


def keep_kernel(weight_ref, out_ref):
    out_ref[...] = weight_ref[...]


def sum_kernel(parts_ref, out_ref):
    sums = parts_ref[0].astype(jnp.float32)
    for index in range(1, NQ):
        sums = sums + parts_ref[index].astype(jnp.float32)
    sums = sums.reshape(NM + 2, CUT, sums.shape[-1])
    shared = jnp.broadcast_to(sums[None, NM:], (NM, 2) + sums.shape[1:])
    packed = jnp.concatenate([sums[:NM, None], shared], axis=1)
    out_ref[...] = packed.reshape(out_ref.shape).astype(out_ref.dtype)


def unpack_kernel(parts_ref, weight_ref, features_ref):
    width = parts_ref.shape[-1]
    parts = parts_ref[...].astype(jnp.float32).reshape(NM, 3, CUT, width)
    features_ref[...] = parts[:, 0].reshape(TILE, width)
    weight_ref[:, :width] = parts[:, 1].reshape(TILE, width)
    weight_ref[:, width:] = parts[:, 2].reshape(TILE, width)


def body(features, weight, upstream, tile_owners, tile_counts, tile_values):
    f32, bf16 = jnp.float32, jnp.bfloat16
    width = features.shape[1]
    values = tile_values[:, 0]
    blocks, slots = values.shape[:2]
    total = blocks * slots
    near = pl.BlockSpec(memory_space=pltpu.VMEM)
    scalar = pl.BlockSpec(memory_space=pltpu.SMEM)
    room = pltpu.CompilerParams(vmem_limit_bytes=4 * 1024 * 1024)

    start = pl.pallas_call(
        start_kernel,
        out_shape=jax.ShapeDtypeStruct((NM, 2 * CUT, width), bf16),
        in_specs=[pl.BlockSpec(memory_space=pl.ANY)] * 3,
        scratch_shapes=[
            pltpu.VMEM((TILE, width), bf16),
            pltpu.SMEM((blocks, slots), jnp.int32),
            pltpu.SMEM((1, blocks), jnp.int32),
            pltpu.SemaphoreType.DMA((3,)),
        ],
        name="start",
    )(features, tile_owners.reshape(blocks, slots), tile_counts.reshape(1, blocks))
    first = swap(exchange(start, NEAR, [[index ^ (NM // 2) for index in range(NM)]]))
    spread = jnp.broadcast_to(first[None, :, :CUT], (NQ, NM, CUT, width)).reshape(NQ, NM * CUT, width)
    table = exchange(spread, "zq", order(AHEAD))
    codes = first[:, CUT, :total].astype(jnp.int32).reshape(NM * total)
    choose = (codes[:, None] == rows_in(AHEAD)[None, :]).astype(bf16)
    pick = (codes[:, None] == rows_in(BACK)[None, :]).astype(bf16)
    halves = jnp.stack([upstream[:, :width], upstream[:, width:]])
    first, halves, weight = lax.optimization_barrier((first, halves, weight))
    upstream_all = lax.all_gather(lax.all_gather(halves, "xh", axis=0), "c", axis=1)
    upstream_all = upstream_all.transpose(0, 1, 3, 2, 4).reshape(blocks * TILE, 2 * width).astype(f32)
    turned = jnp.swapaxes(values, 2, 3)
    weight = pl.pallas_call(
        keep_kernel,
        out_shape=jax.ShapeDtypeStruct(weight.shape, bf16),
        in_specs=[near],
        out_specs=near,
        compiler_params=room,
        name="keep",
    )(weight)
    table, upstream_all, turned, weight, choose, pick = lax.optimization_barrier(
        (table, upstream_all, turned, weight, choose, pick)
    )
    table = table.reshape(NQ * NM, CUT * width)
    wanted = jnp.dot(choose, table, preferred_element_type=f32).astype(bf16)
    third = exchange(wanted.reshape(NM, total, CUT, width), NEAR)
    picked = third.transpose(1, 0, 2, 3).reshape(blocks, slots, TILE, width)
    partial_value = jnp.einsum("btij,btjf->bif", values, picked, preferred_element_type=f32).astype(bf16)
    shared = lax.all_gather(partial_value, REP, axis=0)
    aggregated = add_up(shared).astype(bf16).reshape(blocks * TILE, width)

    pre_act = jnp.dot(aggregated, weight, preferred_element_type=f32)
    hidden_all, pullback = jax.vjp(jax.nn.gelu, pre_act)
    hidden = lax.dynamic_slice_in_dim(hidden_all.astype(bf16), lax.axis_index(REP) * TILE, TILE, 0)
    slope = pullback(upstream_all)[0].astype(bf16)
    weight_part = jnp.dot(aggregated.T, slope, preferred_element_type=f32)
    back_rows = jnp.dot(slope, weight.T, preferred_element_type=f32).astype(bf16).reshape(blocks, TILE, width)
    parts = jnp.einsum("btij,bjf->btif", turned, back_rows, preferred_element_type=f32).astype(bf16)

    parts = parts.reshape(total, NM, CUT, width).transpose(1, 0, 2, 3)
    weight_cut = weight_part.astype(bf16).reshape(NM, CUT, 2, width).transpose(0, 2, 1, 3)
    fifth = exchange(jnp.concatenate([parts, weight_cut], axis=1), NEAR)
    summed = jnp.dot(pick.T, fifth[:, :total].reshape(NM * total, CUT * width), preferred_element_type=f32).astype(bf16)
    weight_sum = add_up(fifth[:, total:]).astype(bf16)
    sixth = exchange(
        jnp.concatenate(
            [
                summed.reshape(NQ, NM, CUT, width),
                jnp.broadcast_to(weight_sum[None], (NQ, 2, CUT, width)),
            ],
            axis=1,
        ).reshape(NQ, (NM + 2) * CUT, width),
        "zq",
        order(BACK),
    )
    packed = pl.pallas_call(
        sum_kernel,
        out_shape=jax.ShapeDtypeStruct((NM, 3 * CUT, width), bf16),
        in_specs=[near],
        out_specs=near,
        compiler_params=room,
        name="sum_far",
    )(sixth)
    last = exchange(packed, NEAR)
    grad_weight, grad_features = pl.pallas_call(
        unpack_kernel,
        out_shape=(jax.ShapeDtypeStruct((TILE, 2 * width), f32), jax.ShapeDtypeStruct((TILE, width), f32)),
        in_specs=[near],
        out_specs=(near, near),
        compiler_params=room,
        name="unpack",
    )(last)
    return (hidden, grad_weight, grad_features)


def solution(mesh):
    parted = Mesh(mesh.devices.reshape(NY, NQ, NZP, NX, 2, 2), ROW + REP)
    in_specs = (
        P(ROW + REP, None),
        P(),
        P(ROW + REP, None),
        P(ROW, REP, None),
        P(ROW, REP),
        P(ROW, REP, None, None, None),
    )
    out_specs = (P(ROW + REP, None), P(), P(ROW + REP, None))
    return jax.shard_map(body, mesh=parted, in_specs=in_specs, out_specs=out_specs, check_vma=False)
```

```python
import jax
import jax.numpy as jnp
from jax import lax
from jax.experimental import pallas as pl
from jax.experimental.pallas import tpu as pltpu
from jax.sharding import Mesh, PartitionSpec as P

ROW = ("y", "zq", "zp", "xl")
REP = ("xh", "c")
NEAR = ("y", "zp", "xl")
NY, NQ, NZP, NX = 4, 8, 2, 2
NM = NY * NZP * NX
TILE = 128
CUT = TILE // NM


AHEAD, BACK = 5, 4


def order(lead):
    return [[(index + lead) % NQ for index in range(NQ)]]


def swap(array):
    return jnp.concatenate([array[NM // 2 :], array[: NM // 2]])


def rows_in(lead):
    place = jnp.arange(NQ * NM, dtype=jnp.int32)
    zq = (place // NM + lead) % NQ
    return ((place // (NZP * NX)) % NY) * (NQ * NZP * NX) + zq * (NZP * NX) + place % (NZP * NX)


def exchange(array, axes, groups=None):
    flat = array.reshape(array.shape[0], -1, array.shape[-1])
    flat = lax.all_to_all(flat, axes, split_axis=0, concat_axis=0, axis_index_groups=groups, tiled=True)
    return flat.reshape(array.shape)


def add_up(terms):
    total = terms[0].astype(jnp.float32)
    for index in range(1, terms.shape[0]):
        total = total + terms[index].astype(jnp.float32)
    return total


def start_kernel(features_in, owners_in, counts_in, out_ref, features_ref, owners_ref, counts_ref, done):
    copies = [
        pltpu.make_async_copy(owners_in, owners_ref, done.at[0]),
        pltpu.make_async_copy(counts_in, counts_ref, done.at[1]),
        pltpu.make_async_copy(features_in, features_ref, done.at[2]),
    ]
    for copy in copies:
        copy.start()
    for copy in copies:
        copy.wait()
    width = features_ref.shape[1]
    blocks, slots = owners_ref.shape
    lane = lax.broadcasted_iota(jnp.int32, (CUT, width), 1)
    code = jnp.full((CUT, width), -1, jnp.int32)
    for block in range(blocks):
        for slot in range(slots):
            wanted = jnp.where(slot < counts_ref[0, block], owners_ref[block, slot], -1)
            code = jnp.where(lane == block * slots + slot, wanted, code)
    code = jnp.broadcast_to(code.astype(jnp.float32)[None], (NM, CUT, width))
    cut = swap(features_ref[...].astype(jnp.float32).reshape(NM, CUT, width))
    out_ref[...] = jnp.concatenate([cut, code], axis=1).astype(out_ref.dtype)


def keep_kernel(weight_ref, out_ref):
    out_ref[...] = weight_ref[...]


def sum_kernel(parts_ref, out_ref):
    sums = parts_ref[0].astype(jnp.float32)
    for index in range(1, NQ):
        sums = sums + parts_ref[index].astype(jnp.float32)
    sums = sums.reshape(NM + 2, CUT, sums.shape[-1])
    shared = jnp.broadcast_to(sums[None, NM:], (NM, 2) + sums.shape[1:])
    packed = jnp.concatenate([sums[:NM, None], shared], axis=1)
    out_ref[...] = packed.reshape(out_ref.shape).astype(out_ref.dtype)


def unpack_kernel(parts_ref, weight_ref, features_ref):
    width = parts_ref.shape[-1]
    parts = parts_ref[...].astype(jnp.float32).reshape(NM, 3, CUT, width)
    features_ref[...] = parts[:, 0].reshape(TILE, width)
    weight_ref[:, :width] = parts[:, 1].reshape(TILE, width)
    weight_ref[:, width:] = parts[:, 2].reshape(TILE, width)


def body(features, weight, upstream, tile_owners, tile_counts, tile_values):
    f32, bf16 = jnp.float32, jnp.bfloat16
    width = features.shape[1]
    values = tile_values[:, 0]
    blocks, slots = values.shape[:2]
    total = blocks * slots
    near = pl.BlockSpec(memory_space=pltpu.VMEM)
    scalar = pl.BlockSpec(memory_space=pltpu.SMEM)
    room = pltpu.CompilerParams(vmem_limit_bytes=4 * 1024 * 1024)

    start = pl.pallas_call(
        start_kernel,
        out_shape=jax.ShapeDtypeStruct((NM, 2 * CUT, width), bf16),
        in_specs=[pl.BlockSpec(memory_space=pl.ANY)] * 3,
        scratch_shapes=[
            pltpu.VMEM((TILE, width), bf16),
            pltpu.SMEM((blocks, slots), jnp.int32),
            pltpu.SMEM((1, blocks), jnp.int32),
            pltpu.SemaphoreType.DMA((3,)),
        ],
        name="start",
    )(features, tile_owners.reshape(blocks, slots), tile_counts.reshape(1, blocks))
    first = swap(exchange(start, NEAR, [[index ^ (NM // 2) for index in range(NM)]]))
    spread = jnp.broadcast_to(first[None, :, :CUT], (NQ, NM, CUT, width)).reshape(NQ, NM * CUT, width)
    table = exchange(spread, "zq", order(AHEAD))
    codes = first[:, CUT, :total].astype(jnp.int32).reshape(NM * total)
    choose = (codes[:, None] == rows_in(AHEAD)[None, :]).astype(bf16)
    pick = (codes[:, None] == rows_in(BACK)[None, :]).astype(bf16)
    halves = jnp.stack([upstream[:, :width], upstream[:, width:]])
    first, halves, weight = lax.optimization_barrier((first, halves, weight))
    upstream_all = lax.all_gather(lax.all_gather(halves, "c", axis=0), "xh", axis=0)
    upstream_all = upstream_all.transpose(0, 1, 3, 2, 4).reshape(blocks * TILE, 2 * width).astype(f32)
    turned = jnp.swapaxes(values, 2, 3)
    weight = pl.pallas_call(
        keep_kernel,
        out_shape=jax.ShapeDtypeStruct(weight.shape, bf16),
        in_specs=[near],
        out_specs=near,
        compiler_params=room,
        name="keep",
    )(weight)
    table, upstream_all, turned, weight, choose, pick = lax.optimization_barrier(
        (table, upstream_all, turned, weight, choose, pick)
    )
    table = table.reshape(NQ * NM, CUT * width)
    wanted = jnp.dot(choose, table, preferred_element_type=f32).astype(bf16)
    third = exchange(wanted.reshape(NM, total, CUT, width), NEAR)
    picked = third.transpose(1, 0, 2, 3).reshape(blocks, slots, TILE, width)
    partial_value = jnp.einsum("btij,btjf->bif", values, picked, preferred_element_type=f32).astype(bf16)
    shared = lax.all_gather(partial_value, REP, axis=0)
    aggregated = add_up(shared).astype(bf16).reshape(blocks * TILE, width)

    pre_act = jnp.dot(aggregated, weight, preferred_element_type=f32)
    hidden_all, pullback = jax.vjp(jax.nn.gelu, pre_act)
    hidden = lax.dynamic_slice_in_dim(hidden_all.astype(bf16), lax.axis_index(REP) * TILE, TILE, 0)
    slope = pullback(upstream_all)[0].astype(bf16)
    weight_part = jnp.dot(aggregated.T, slope, preferred_element_type=f32)
    back_rows = jnp.dot(slope, weight.T, preferred_element_type=f32).astype(bf16).reshape(blocks, TILE, width)
    parts = jnp.einsum("btij,bjf->btif", turned, back_rows, preferred_element_type=f32).astype(bf16)

    parts = parts.reshape(total, NM, CUT, width).transpose(1, 0, 2, 3)
    weight_cut = weight_part.astype(bf16).reshape(NM, CUT, 2, width).transpose(0, 2, 1, 3)
    fifth = exchange(jnp.concatenate([parts, weight_cut], axis=1), NEAR)
    summed = jnp.dot(pick.T, fifth[:, :total].reshape(NM * total, CUT * width), preferred_element_type=f32).astype(bf16)
    weight_sum = add_up(fifth[:, total:]).astype(bf16)
    sixth = exchange(
        jnp.concatenate(
            [
                summed.reshape(NQ, NM, CUT, width),
                jnp.broadcast_to(weight_sum[None], (NQ, 2, CUT, width)),
            ],
            axis=1,
        ).reshape(NQ, (NM + 2) * CUT, width),
        "zq",
        order(BACK),
    )
    packed = pl.pallas_call(
        sum_kernel,
        out_shape=jax.ShapeDtypeStruct((NM, 3 * CUT, width), bf16),
        in_specs=[near],
        out_specs=near,
        compiler_params=room,
        name="sum_far",
    )(sixth)
    last = exchange(packed, NEAR)
    grad_weight, grad_features = pl.pallas_call(
        unpack_kernel,
        out_shape=(jax.ShapeDtypeStruct((TILE, 2 * width), f32), jax.ShapeDtypeStruct((TILE, width), f32)),
        in_specs=[near],
        out_specs=(near, near),
        compiler_params=room,
        name="unpack",
    )(last)
    return (hidden, grad_weight, grad_features)


def solution(mesh):
    parted = Mesh(mesh.devices.reshape(NY, NQ, NZP, NX, 2, 2), ROW + REP)
    in_specs = (
        P(ROW + REP, None),
        P(),
        P(ROW + REP, None),
        P(ROW, REP, None),
        P(ROW, REP),
        P(ROW, REP, None, None, None),
    )
    out_specs = (P(ROW + REP, None), P(), P(ROW + REP, None))
    return jax.shard_map(body, mesh=parted, in_specs=in_specs, out_specs=out_specs, check_vma=False)
```
